256 devices in a mesh: blk: 8 (over y, core), req: 32 (over z, x).
Axes of the slice: x: 4, y: 4, z: 8, core: 2. Of those that a mesh axis runs over, the one named last changes fastest.
Arguments:
- hidden: bfloat16 [12288, 8192], P('req', 'blk'), may hold values from -120 to 120
- input_norm_gain: float32 [8192], replicated, may hold values from 0.1 to 1.9
- query_weight: bfloat16 [8192, 8192], P('req', 'blk')
- keyvalue_weight: bfloat16 [8192, 2048], P('req', 'blk')
- adapter_down: bfloat16 [32, 3, 16, 8192], P('req', None, None, 'blk'), may hold values from -0.0625 to 0.0625
- adapter_up_query: bfloat16 [32, 16, 8192], P('req', None, 'blk'), may hold values from -1.5 to 1.5
- adapter_up_keyvalue: bfloat16 [32, 16, 2048], P('req', None, 'blk'), may hold values from -1.5 to 1.5
- packed_lengths: int32 [32, 4], P('req'), may hold values from 1 to 192, 384 in all within a row
- prompt_adapter: int32 [32, 4], P('req'), may hold values from 0 to 31
Outputs:
- context: bfloat16 [12288, 8192], P('req', 'blk')
- key_cache: bfloat16 [12288, 1024], P('req', 'blk')
- value_cache: bfloat16 [12288, 1024], P('req', 'blk')
The draws below stay inside these ranges and needn't reach their ends.
Inputs may be any that keep to these rules, and one draw needn't show every extreme that they name: `packed_lengths`: each row sums to 384; the longest prompt of the whole draw has 192 tokens.
All inputs are finite; a program needn't handle non-finite values.
Results may differ from the reference program's by a relative error of at most 0.012.
The reference program's roundings to bfloat16 on the way (of `normed`, `low_rank` and `attend`) count: a program that leaves them out, or rounds other values in their place, can miss the bound.
Values may be sent and summed in bfloat16 or wider, within the bound.
A program may use at most 128 MiB of HBM per device.

```python
import math
import jax
import jax.numpy as jnp
import numpy as np
from jax import lax

MODEL_WIDTH = 8192
HEAD_WIDTH = 128
QUERY_LOCAL = 8
KEYVALUE_LOCAL = 1
ADAPTER_RANK = 16
PROMPTS_PER_REQ = 4
TOKEN_SLOTS = 384
LONGEST = 192
QUERY_HEADS = 64
KEYVALUE_HEADS = 8
ADAPTER_TOTAL = 32
TOKENS = 12288
N_BLK = 8
N_REQ = 32


def draw_hidden(key, part):
    streams = jax.random.split(key, 3)
    row_scale = jnp.exp(jax.random.uniform(streams[0], (TOKENS, 1), minval=0.0, maxval=math.log(10.0)))
    column_scale = jnp.exp(jax.random.uniform(streams[1], (1, MODEL_WIDTH), minval=0.0, maxval=math.log(10.0)))
    noise = jnp.clip(jax.random.normal(streams[2], (TOKENS, MODEL_WIDTH)), -4.0, 4.0)
    result = noise * row_scale * column_scale * 0.3
    return result.astype(jnp.bfloat16)


def draw_query_weight(key, part):
    base = jnp.clip(jax.random.normal(jax.random.fold_in(key, 11), (MODEL_WIDTH, QUERY_HEADS * HEAD_WIDTH)), -6.0, 6.0) * MODEL_WIDTH ** (-0.5)
    return base.astype(jnp.bfloat16)


def draw_keyvalue_weight(key, part):
    base = jnp.clip(jax.random.normal(jax.random.fold_in(key, 12), (MODEL_WIDTH, 2 * KEYVALUE_HEADS * HEAD_WIDTH)), -6.0, 6.0) * MODEL_WIDTH ** (-0.5)
    return base.astype(jnp.bfloat16)


def plant(values, rng, low, largest):
    shape = values.shape
    spot = [jax.random.randint(jax.random.fold_in(rng, axis), (), 0, shape[axis]) for axis in range(len(shape))]
    values = values.at[tuple(spot)].set(low)
    longest = shape.index(max(shape))
    spot[longest] = (spot[longest] + 1) % shape[longest]
    return values.at[tuple(spot)].set(largest)


def steps_of(rng, shape, pieces, smallest, largest):
    gain = 1.0
    for axis_at, parts in pieces:
        heights = jax.random.uniform(jax.random.fold_in(jax.random.fold_in(rng, 6), axis_at), (parts,), jnp.float32, smallest / len(pieces), largest / len(pieces))
        gain = gain * jnp.repeat(jnp.exp(heights), shape[axis_at] // parts).reshape((-1,) + (1,) * (len(shape) - 1 - axis_at))
    return gain


def profile(count, total, limit, slope):
    loads = [(1 << 20) // math.isqrt(standing ** slope) + 1 for standing in range(2, count + 1)]
    rest, counts = total - limit - (count - 1), [1] * (count - 1)
    while rest > 0:
        candidates = [i for i in range(count - 1) if counts[i] < limit]
        pool, remaining = sum([loads[i] for i in candidates]), rest
        for i in candidates:
            more = min(limit - counts[i], max(1, remaining * loads[i] // pool), rest)
            counts[i] = counts[i] + more
            rest = rest - more
    return np.array([limit] + counts)


def uneven_parts(stream_key, count, total, bound, slope):
    if count == 2:
        one = jax.random.randint(stream_key, (), max(1, total - bound), min(bound, total - 1) + 1)
        return jnp.stack([one, total - one])
    sizes = jnp.asarray(profile(count, total, bound, slope), jnp.int32)
    twos = (count - 1) // 2
    donor, receiver = sizes[1:1 + 2 * twos:2], sizes[2:2 + 2 * twos:2]
    slack = jnp.minimum(donor - 1, bound - receiver)
    passed = jax.random.randint(jax.random.fold_in(stream_key, 1), (twos,), 0, 1 << 20) % (slack + 1)
    sizes = sizes.at[1:1 + 2 * twos:2].set(donor - passed).at[2:2 + 2 * twos:2].set(receiver + passed)
    return sizes[jax.random.permutation(jax.random.fold_in(stream_key, 2), count)]


def gaussian(own_key, extent, deviation, limit, pieces=(), kind=jnp.bfloat16):
    values = jax.random.normal(own_key, extent, jnp.float32) * deviation
    if len(pieces) > 0:
        values = steps_of(own_key, extent, pieces, -0.22, 0.18) * values
    return jnp.clip(values, min=-limit, max=limit).astype(kind)


def setup_inputs(seed: int = 0) -> dict:
    seeds = jax.random.split(jax.random.key(seed), 10)
    return {
        "hidden": draw_hidden(jax.random.fold_in(seeds[9], 71), 0),
        "input_norm_gain": jnp.clip(1.0 + 0.18 * jax.random.normal(seeds[1], (MODEL_WIDTH,), jnp.float32), 0.1, 1.9),
        "query_weight": draw_query_weight(jax.random.fold_in(seeds[9], 71), 0),
        "keyvalue_weight": draw_keyvalue_weight(jax.random.fold_in(seeds[9], 71), 0),
        "adapter_down": gaussian(seeds[4], (ADAPTER_TOTAL, 3, ADAPTER_RANK, MODEL_WIDTH), MODEL_WIDTH ** -0.5, 0.0625, ((0, 32), (3, 8))),
        "adapter_up_query": gaussian(seeds[5], (ADAPTER_TOTAL, ADAPTER_RANK, QUERY_HEADS * HEAD_WIDTH), ADAPTER_RANK ** -0.5, 1.5, ((0, 32), (2, 8))),
        "adapter_up_keyvalue": gaussian(seeds[6], (ADAPTER_TOTAL, ADAPTER_RANK, 2 * KEYVALUE_HEADS * HEAD_WIDTH), ADAPTER_RANK ** -0.5, 1.5, ((0, 32), (2, 8))),
        "packed_lengths": jax.vmap(lambda own: uneven_parts(own, PROMPTS_PER_REQ, TOKEN_SLOTS, LONGEST, 2))(jax.random.split(seeds[7], N_REQ)).reshape((N_REQ, PROMPTS_PER_REQ)).astype(jnp.int32),
        "prompt_adapter": plant(jax.random.randint(seeds[8], (N_REQ, PROMPTS_PER_REQ), 0, ADAPTER_TOTAL), jax.random.fold_in(seeds[8], 1), 0, ADAPTER_TOTAL - 1).astype(jnp.int32),
    }


epsilon = 1e-05
adapter_scale = 2.0
rope_base = 10000.0

def apply_rotation(vectors, cosine_table, sine_table):
    half_size = vectors.shape[-1] // 2
    first_half = vectors[..., :half_size]
    second_half = vectors[..., half_size:]
    turned = jnp.concatenate([-second_half, first_half], axis=-1)
    return vectors * cosine_table + turned * sine_table

def layout(lengths, count):
    slot_index = jnp.arange(count, dtype=jnp.int32)
    prompt_ends = jnp.cumsum(lengths).astype(jnp.int32)
    prompt_starts = (prompt_ends - lengths).astype(jnp.int32)
    member = (slot_index[:, None] >= prompt_starts[None, :]) & (slot_index[:, None] < prompt_ends[None, :])
    position = lax.optimization_barrier(jnp.sum(jnp.where(member, slot_index[:, None] - prompt_starts[None, :], 0), axis=1)).astype(jnp.int32)
    owner = lax.optimization_barrier(jnp.sum((slot_index[:, None] >= prompt_ends[None, :]).astype(jnp.int32), axis=1)).astype(jnp.int32)
    return (member.astype(jnp.float32), position, owner, slot_index)

def rope_tables(position, head_size):
    frequency = rope_base ** (-(jnp.arange(head_size // 2, dtype=jnp.float32) * 2.0 / head_size))
    angles = position.astype(jnp.float32)[:, None] * frequency[None, :]
    cosine_table = jnp.cos(angles)
    sine_table = jnp.sin(angles)
    return (jnp.concatenate([cosine_table, cosine_table], 1)[:, None, :], jnp.concatenate([sine_table, sine_table], 1)[:, None, :])

def attention(query_states, key_vectors, value_vectors, owner, slot_index):
    scores = jnp.einsum('tkgc,skc->kgts', query_states.astype(jnp.float32), key_vectors.astype(jnp.float32))
    scores = scores / math.sqrt(HEAD_WIDTH)
    allowed = (owner[:, None] == owner[None, :]) & (slot_index[None, :] <= slot_index[:, None])
    scores = jnp.where(allowed[None, None], scores, -1e+30)
    row_max = lax.optimization_barrier(jnp.max(scores, axis=-1, keepdims=True))
    exponent = jnp.exp(scores - row_max)
    attend = (exponent / lax.optimization_barrier(jnp.sum(exponent, axis=-1, keepdims=True))).astype(jnp.bfloat16)
    return jnp.einsum('kgts,skc->tkgc', attend.astype(jnp.float32), value_vectors.astype(jnp.float32))

def reference(hidden, input_norm_gain, query_weight, keyvalue_weight, adapter_down, adapter_up_query, adapter_up_keyvalue, packed_lengths, prompt_adapter):
    keyvalue_heads = KEYVALUE_LOCAL * N_BLK
    query_head_rows = QUERY_LOCAL * N_BLK

    def one_group(group_data):
        row_block, lengths, picked_adapter = group_data
        member, position, owner, slot_index = layout(lengths, TOKEN_SLOTS)
        values = row_block.astype(jnp.float32)
        mean_square = lax.optimization_barrier(jnp.mean(values * values, axis=1, keepdims=True))
        normed = (values * lax.rsqrt(mean_square + epsilon) * input_norm_gain[None, :]).astype(jnp.bfloat16)
        query_plain = jnp.dot(normed, query_weight, preferred_element_type=jnp.float32)
        base_pair = jnp.dot(normed, keyvalue_weight, preferred_element_type=jnp.float32)
        down_selected = adapter_down[picked_adapter].astype(jnp.float32)
        rank_all = jnp.einsum('td,pjrd->tpjr', normed.astype(jnp.float32), down_selected)
        low_rank = lax.optimization_barrier(jnp.sum(rank_all * member[:, :, None, None], axis=1)).astype(jnp.bfloat16)
        low_rank = lax.optimization_barrier(low_rank).astype(jnp.float32)
        up_query_selected = adapter_up_query[picked_adapter].astype(jnp.float32)
        query_update = lax.optimization_barrier(jnp.sum(jnp.einsum('tr,prc->tpc', low_rank[:, 0], up_query_selected) * member[:, :, None], axis=1))
        up_keyvalue_selected = adapter_up_keyvalue[picked_adapter].astype(jnp.float32).reshape(PROMPTS_PER_REQ, ADAPTER_RANK, keyvalue_heads, 2, HEAD_WIDTH)
        key_update = lax.optimization_barrier(jnp.sum(jnp.einsum('tr,prhc->tphc', low_rank[:, 1], up_keyvalue_selected[:, :, :, 0]) * member[:, :, None, None], axis=1))
        value_update = lax.optimization_barrier(jnp.sum(jnp.einsum('tr,prhc->tphc', low_rank[:, 2], up_keyvalue_selected[:, :, :, 1]) * member[:, :, None, None], axis=1))
        cosine_table, sine_table = rope_tables(position, HEAD_WIDTH)
        query_complete = query_plain.reshape(TOKEN_SLOTS, query_head_rows, HEAD_WIDTH) + adapter_scale * query_update.reshape(TOKEN_SLOTS, query_head_rows, HEAD_WIDTH)
        query_states = apply_rotation(query_complete, cosine_table, sine_table).astype(jnp.bfloat16)
        keyvalue_plain = base_pair.reshape(TOKEN_SLOTS, keyvalue_heads, 2, HEAD_WIDTH)
        key_vectors = apply_rotation(keyvalue_plain[:, :, 0] + adapter_scale * key_update, cosine_table, sine_table).astype(jnp.bfloat16)
        value_vectors = (keyvalue_plain[:, :, 1] + adapter_scale * value_update).astype(jnp.bfloat16)
        grouped = query_states.reshape(TOKEN_SLOTS, keyvalue_heads, QUERY_LOCAL, HEAD_WIDTH)
        context = attention(grouped, key_vectors, value_vectors, owner, slot_index).astype(jnp.bfloat16)
        return (context.reshape(TOKEN_SLOTS, query_head_rows * HEAD_WIDTH), key_vectors.reshape(TOKEN_SLOTS, keyvalue_heads * HEAD_WIDTH), value_vectors.reshape(TOKEN_SLOTS, keyvalue_heads * HEAD_WIDTH))
    context, key_cache, value_cache = lax.map(one_group, (hidden.reshape(N_REQ, TOKEN_SLOTS, MODEL_WIDTH), packed_lengths, prompt_adapter))
    return (context.reshape(N_REQ * TOKEN_SLOTS, query_head_rows * HEAD_WIDTH), key_cache.reshape(N_REQ * TOKEN_SLOTS, keyvalue_heads * HEAD_WIDTH), value_cache.reshape(N_REQ * TOKEN_SLOTS, keyvalue_heads * HEAD_WIDTH))
```

```python
import functools
import math

import jax
import jax.numpy as jnp
import numpy as np
from jax import lax
from jax.experimental import pallas as pl
from jax.experimental.pallas import tpu as pltpu
from jax.sharding import PartitionSpec as P

EPSILON = 1e-05
ADAPTER_SCALE = 2.0
ROPE_BASE = 10000.0
HEAD = 128
T = 384
RANK = 16
NZ, NX, NY = 8, 4, 4
WIDTH = 8192
BF, F32 = jnp.bfloat16, jnp.float32

ITEM_UP, ITEM_W0, ITEM_DOWN, ITEM_W1, ITEM_W2, ITEM_W3, ITEM_W4 = range(7)
W_ITEMS = (ITEM_W0, ITEM_W1, ITEM_W2, ITEM_W3, ITEM_W4)


def kernel(
    hid, gain, qw, kvw, down, up_q, up_kv, freq, lens, picks,
    ctx_o, key_o, val_o,
    wg, act, nrm, dg, ug, ssb, avb,
    relay_s, relay_r, fin_s, fin_r, own, hold,
    lrx_s, lrx_r, lrc_s, lrc_r, lry_s, lry_r,
    lhs, bias, cosb, sinb, keys, vals,
    z_send, z_recv, y_send, y_recv, xa_send, xa_recv, xu_send, xu_recv,
    av_send, av_recv, ss_send, ss_recv, d1_send, d1_recv,
    rs_send, rs_recv, lr_send, lr_recv, loc_sem,
):
    b = lax.axis_index("blk")
    r = lax.axis_index("req")
    y, c = lax.div(b, 2), lax.rem(b, 2)
    z, x = lax.div(r, 4), lax.rem(r, 4)
    sgn = 1 - 2 * c

    def dev(zz, xx, yy, cc):
        return {"blk": yy * 2 + cc, "req": zz * 4 + xx}

    def zrel(d):
        return lax.rem(z + d + NZ, NZ)

    def xrel(d):
        return lax.rem(x + d + NX, NX)

    def yrel(d):
        return lax.rem(y + d + NY, NY)

    def remote(src, dst, ssem, rsem, to):
        return pltpu.make_async_remote_copy(
            src_ref=src, dst_ref=dst, send_sem=ssem, recv_sem=rsem,
            device_id=to, device_id_type=pl.DeviceIdType.MESH,
        )

    sent = []

    def go(copy):
        copy.start()
        sent.append(copy)

    def mo(v, m):
        return pl.multiple_of(v, m)

    barrier = pltpu.get_barrier_semaphore()
    peers = [dev(z, xrel(dx), yrel(dy), c) for dx in range(4) for dy in range(4) if dx or dy]
    peers += [dev(z, x, yrel(dy), 1 - c) for dy in range(4)]
    peers += [dev(zrel(1), x, y, c), dev(zrel(-1), x, y, c)]
    for peer in peers:
        pl.semaphore_signal(barrier, inc=1, device_id=peer, device_id_type=pl.DeviceIdType.MESH)

    def krow(q):
        return lax.rem(q, 2) * 4 + lax.div(q, 2)

    own_rows = pl.ds(mo(krow(z) * 256, 256), 256)
    wg[0, own_rows, :] = kvw[...]
    for i in range(4):
        wg[1 + i, own_rows, :] = qw[:, i * 256:(i + 1) * 256]
    up_rows = pl.ds(mo(z * 16, 16), 16)
    ug[up_rows, 0:256] = up_kv[...]
    ug[up_rows, 256:1280] = up_q[...]

    acc = None
    for i in range(8):
        v = hid[:, i * 128:(i + 1) * 128].astype(F32)
        acc = v * v if acc is None else acc + v * v
    ssb[b] = jnp.broadcast_to(jnp.sum(acc.T, axis=0, keepdims=True), (8, T))

    l0, l1, l2 = lens[0, 0], lens[0, 1], lens[0, 2]
    e0, e1, e2 = l0, l0 + l1, l0 + l1 + l2
    row_t = lax.broadcasted_iota(jnp.int32, (8, T), 1)

    def pick(t, v0, v1, v2, v3):
        return jnp.where(t < e0, v0, jnp.where(t < e1, v1, jnp.where(t < e2, v2, v3)))

    avb[0] = pick(row_t, picks[0, 0], picks[0, 1], picks[0, 2], picks[0, 3]).astype(F32)

    pl.semaphore_wait(barrier, len(peers))

    def z_slot(item, h, q):
        if item == ITEM_UP:
            return ug.at[pl.ds(mo(q * 16, 16), 16), :]
        if item == ITEM_DOWN:
            return dg.at[q]
        return wg.at[W_ITEMS.index(item), pl.ds(mo(krow(q) * 256 + h * 128, 128), 128), :]

    def z_copy(item, h, d, step):
        way = sgn if d == 0 else -sgn
        ref = z_slot(item, h, lax.rem(z - way * (step - 1) + NZ, NZ))
        n = ((item * 2 + h) * 2 + d) * 4 + step - 1
        return remote(ref, ref, z_send.at[n], z_recv.at[n], dev(lax.rem(z + way + NZ, NZ), x, y, c))

    def z_wait(item, h, d, step):
        way = sgn if d == 0 else -sgn
        ref = z_slot(item, h, lax.rem(z - way * step + NZ, NZ))
        n = ((item * 2 + h) * 2 + d) * 4 + step - 1
        remote(ref, ref, z_send.at[n], z_recv.at[n], dev(lax.rem(z + way + NZ, NZ), x, y, c)).wait_recv()

    def halves(item):
        return (0,) if item in (ITEM_UP, ITEM_DOWN) else (0, 1)

    def z_start(item):
        for h in halves(item):
            for d in (0, 1):
                go(z_copy(item, h, d, 1))

    def z_step(item, step, hs=None):
        for h in halves(item) if hs is None else hs:
            for d in (0, 1):
                if step == 4 and d == 1:
                    continue
                z_wait(item, h, d, step)
                if step < 3 or (step == 3 and d == 0):
                    go(z_copy(item, h, d, step + 1))

    for p in range(1, 8):
        dy, dc = p // 2, p % 2
        go(remote(ssb.at[b], ssb.at[b], ss_send.at[p], ss_recv.at[p],
                  dev(z, x, yrel(dy), lax.rem(c + dc, 2))))
    z_start(ITEM_UP)
    for d in range(4):
        def copy(d=d):
            return remote(
                down.at[:, pl.ds(mo(xrel(d) * 256, 256), 256)],
                dg.at[z, :, pl.ds(mo(y * 256, 256), 256)],
                d1_send.at[d], d1_recv.at[y], dev(z, xrel(d), x, c))
        if d:
            go(copy())
        else:
            @pl.when(y == x)
            def _():
                pltpu.make_async_copy(
                    down.at[:, pl.ds(mo(x * 256, 256), 256)],
                    dg.at[z, :, pl.ds(mo(y * 256, 256), 256)], d1_recv.at[y]).start()

            @pl.when(y != x)
            def _():
                copy().start()
    z_start(ITEM_W0)
    for d in range(1, 4):
        go(remote(avb.at[0], avb.at[(4 - d) % 4], av_send.at[d], av_recv.at[d], dev(z, xrel(d), y, c)))

    col_t = lax.broadcasted_iota(jnp.int32, (T, HEAD), 0)
    position = col_t - pick(col_t, 0, e0, e1, e2)
    angles = position.astype(F32) * freq[0:1, :]
    cosb[...] = jnp.cos(angles)
    lane = lax.broadcasted_iota(jnp.int32, (T, HEAD), 1)
    sines = jnp.sin(angles)
    sinb[...] = jnp.where(lane < HEAD // 2, -sines, sines)

    z_step(ITEM_UP, 1)

    for p in range(1, 8):
        dy, dc = p // 2, p % 2
        q = yrel(-dy) * 2 + lax.rem(c + dc, 2)
        remote(ssb.at[q], ssb.at[q], ss_send.at[p], ss_recv.at[p],
               dev(z, x, yrel(dy), lax.rem(c + dc, 2))).wait_recv()
    total = ssb[0]
    for i in range(1, 8):
        total = total + ssb[i]
    factor = lax.rsqrt(total / WIDTH + EPSILON)
    factor = jnp.broadcast_to(factor[0:1, :], (HEAD, T)).T
    gains = gain[pl.ds(mo(b * 8, 8), 8), :]
    for i in range(8):
        v = hid[:, i * 128:(i + 1) * 128].astype(F32)
        nrm[:, i * 128:(i + 1) * 128] = (v * factor * gains[i:i + 1, :]).astype(BF)

    own_cols = pl.ds(mo((c * 4 + y) * 256, 256), 256)
    quarter = pl.ds(mo(x * 256, 256), 256)

    def xa(d):
        return remote(
            nrm.at[:, pl.ds(mo(xrel(d) * 256, 256), 256)], act.at[(4 - d) % 4, :, own_cols],
            xa_send.at[d], xa_recv.at[d], dev(z, xrel(d), y, c))

    def y_cols(yy):
        return pl.ds(mo((c * 4 + yy) * 256, 256), 256)

    def y_copy(k, n):
        if n < 2:
            src = nrm.at[:, quarter] if k == 0 else act.at[k, :, own_cols]
            dst = act.at[k, :, own_cols]
            to = dev(z, x, yrel(1 - 2 * n), c)
        elif n == 2:
            src = dst = act.at[k, 0:192, y_cols(yrel(-1))]
            to = dev(z, x, yrel(1), c)
        elif n == 3:
            src = dst = act.at[k, 192:384, y_cols(yrel(1))]
            to = dev(z, x, yrel(-1), c)
        else:
            src = dst = act.at[k, :, pl.ds(mo(c * 1024, 1024), 1024)]
            to = dev(z, x, y, 1 - c)
        return remote(src, dst, y_send.at[k * 5 + n], y_recv.at[k * 5 + n], to)

    def y_wait(k, n):
        if n < 2:
            dst = act.at[k, :, y_cols(yrel(2 * n - 1))]
        elif n == 2:
            dst = act.at[k, 0:192, y_cols(yrel(2))]
        elif n == 3:
            dst = act.at[k, 192:384, y_cols(yrel(2))]
        else:
            dst = act.at[k, :, pl.ds(mo((1 - c) * 1024, 1024), 1024)]
        remote(dst, dst, y_send.at[k * 5 + n], y_recv.at[k * 5 + n], dev(z, x, y, 1 - c)).wait_recv()

    own_copy = pltpu.make_async_copy(nrm.at[:, quarter], act.at[0, :, own_cols], loc_sem.at[0])

    def y_begin(k):
        if k:
            xa_k = remote(act.at[k, :, own_cols], act.at[k, :, own_cols], xa_send.at[4 - k], xa_recv.at[4 - k],
                          dev(z, xrel(1), y, c))
            xa_k.wait_recv()
        for n in (0, 1):
            go(y_copy(k, n))

    def y_middle(k):
        for n in (0, 1):
            y_wait(k, n)
            go(y_copy(k, n + 2))

    def y_end(k):
        for n in (2, 3):
            y_wait(k, n)
        if k == 0:
            own_copy.wait()
        go(y_copy(k, 4))

    def y_done(k):
        y_wait(k, 4)

    y_begin(0)
    for d in (2, 1, 3):
        go(xa(d))
    own_copy.start()

    def xu(d):
        return remote(ug.at[0:128, :], ug.at[pl.ds(((4 - d) % 4) * 128, 128), :],
                      xu_send.at[d], xu_recv.at[d], dev(z, xrel(d), y, c))

    def lrx(k):
        return remote(lrx_s.at[k], lrx_r.at[k], lr_send.at[k], lr_recv.at[k], dev(z, xrel(k), y, c))

    def low_partial(k):
        part = lax.dot_general(
            dg[...].reshape(NZ * 48, 1024), act[k, :, pl.ds(mo(c * 1024, 1024), 1024)],
            (((1,), (1,)), ((), ())), preferred_element_type=F32)
        ids = avb[k, 0:1, :]
        out = None
        for q in range(NZ):
            hit = ids == (4 * q + y).astype(F32)
            term = jnp.where(hit, part[q * 48:(q + 1) * 48, :], 0.0)
            out = term if out is None else out + term
        lrx_s[k] = out
        if k:
            go(lrx(k))

    def low_core():
        total = lrx_s[0]
        for k in range(1, 4):
            lrx(k).wait_recv()
            total = total + lrx_r[k]
        lrc_s[...] = total
        go(remote(lrc_s, lrc_r, lr_send.at[4], lr_recv.at[4], dev(z, x, y, 1 - c)))

    def lry(d):
        return remote(lry_s, lry_r.at[d], lr_send.at[4 + d], lr_recv.at[4 + d], dev(z, x, yrel(d), c))

    def low_y():
        remote(lrc_s, lrc_r, lr_send.at[4], lr_recv.at[4], dev(z, x, y, 1 - c)).wait_recv()
        lry_s[...] = lrc_s[...] + lrc_r[...]
        for d in range(1, 4):
            go(lry(d))

    def low_end():
        total = lry_s[...]
        for d in range(1, 4):
            lry(d).wait_recv()
            total = total + lry_r[d]
        low = total.astype(BF)
        row = lax.broadcasted_iota(jnp.int32, (512, RANK), 0)
        rank = lax.broadcasted_iota(jnp.int32, (512, RANK), 1)
        repeat = ((row & 15) == rank).astype(BF)
        row = lax.broadcasted_iota(jnp.int32, (512, T), 0)
        adapter = 4 * ((row & 127) >> 4) + ((x + (row >> 7)) & 3)
        hit = adapter.astype(F32) == avb[0, 0:1, :]
        for j in range(3):
            spread = jnp.dot(repeat, low[j * RANK:(j + 1) * RANK, :], preferred_element_type=F32)
            lhs[j] = jnp.where(hit, spread, 0.0).T.astype(BF)

    def make_bias():
        tc = lax.broadcasted_iota(jnp.int32, (T, T), 0)
        tr = lax.broadcasted_iota(jnp.int32, (T, T), 1)
        allowed = (pick(tc, 0, 1, 2, 3) == pick(tr, 0, 1, 2, 3)) & (tr <= tc)
        bias[...] = jnp.where(allowed, 0.0, -1e30)

    def part(k, j):
        return jnp.dot(act[k], wg[j], preferred_element_type=F32)

    def relay(j, d):
        return remote(relay_s.at[j, d], relay_r.at[j, d], rs_send.at[j * 4 + d], rs_recv.at[j * 4 + d],
                      dev(z, xrel(1 - 2 * d), y, c))

    def final(j, d):
        return remote(fin_s.at[j, d], fin_r.at[j, d], rs_send.at[j * 4 + 2 + d], rs_recv.at[j * 4 + 2 + d],
                      dev(z, xrel(1 - 2 * d), y, c))

    def rs_far(j):
        p = part(2, j).astype(BF)
        for d in (0, 1):
            relay_s[j, d] = p[d * 192:(d + 1) * 192]
            go(relay(j, d))

    def rs_hold(j, d):
        hold[d] = part(1 if d == 0 else 3, j)

    def rs_near(j, d):
        relay(j, d).wait_recv()
        lo = d * 192
        fin_s[j, d, lo:lo + 192] = (hold[d, lo:lo + 192] + relay_r[j, d].astype(F32)).astype(BF)
        fin_s[j, d, 192 - lo:384 - lo] = hold[d, 192 - lo:384 - lo].astype(BF)
        go(final(j, d))

    def rs_own(j):
        own[...] = part(0, j)

    def rotate(v):
        return v * cosb[...] + pltpu.roll(v, HEAD // 2, axis=1) * sinb[...]

    def chunk_end(j):
        base = own[...]
        for d in (0, 1):
            final(j, d).wait_recv()
            base = base + fin_r[j, d].astype(F32)
        ups = ug[:, j * 256:(j + 1) * 256]
        if j == 0:
            k = base[:, 0:128] + ADAPTER_SCALE * jnp.dot(lhs[1], ups[:, 0:128], preferred_element_type=F32)
            v = base[:, 128:256] + ADAPTER_SCALE * jnp.dot(lhs[2], ups[:, 128:256], preferred_element_type=F32)
            k, v = rotate(k).astype(BF), v.astype(BF)
            keys[...] = k
            vals[...] = v
            key_o[...] = k
            val_o[...] = v
            return
        base = base + ADAPTER_SCALE * jnp.dot(lhs[0], ups, preferred_element_type=F32)
        for i in range(2):
            q = rotate(base[:, i * 128:(i + 1) * 128]).astype(BF)
            head = ((j - 1) * 2 + i) * 128
            for n in range(3):
                rows, wide = slice(n * 128, (n + 1) * 128), (n + 1) * 128
                s = lax.dot_general(q[rows], keys[0:wide, :], (((1,), (1,)), ((), ())),
                                    preferred_element_type=F32)
                s = s * (1.0 / math.sqrt(HEAD)) + bias[rows, 0:wide]
                e = jnp.exp(s - jnp.max(s, axis=1, keepdims=True))
                a = (e / jnp.sum(e, axis=1, keepdims=True)).astype(BF)
                o = jnp.dot(a, vals[0:wide, :], preferred_element_type=F32)
                ctx_o[rows, head:head + 128] = o.astype(BF)

    z_step(ITEM_W0, 1)
    z_step(ITEM_UP, 2)
    z_step(ITEM_W0, 2)
    for q in range(4):
        ref = dg.at[z, :, q * 256:(q + 1) * 256]
        remote(ref, ref, d1_send.at[0], d1_recv.at[q], dev(z, xrel(1), y, c)).wait_recv()
    z_start(ITEM_DOWN)
    y_middle(0)
    z_step(ITEM_UP, 3)
    z_step(ITEM_W0, 3)
    z_start(ITEM_W1)
    y_end(0)
    y_begin(2)
    z_step(ITEM_UP, 4)
    for d in (1, 3, 2):
        go(xu(d))
    y_begin(1)
    y_begin(3)
    z_step(ITEM_DOWN, 1)
    z_step(ITEM_W0, 4)
    make_bias()
    z_step(ITEM_W1, 1)
    y_done(0)
    z_step(ITEM_DOWN, 2)
    y_middle(2)
    z_step(ITEM_W1, 2)
    y_end(2)
    y_middle(1)
    z_step(ITEM_DOWN, 3)
    z_step(ITEM_W1, 3, (0,))
    z_step(ITEM_W1, 3, (1,))
    z_start(ITEM_W2)
    y_end(1)
    z_step(ITEM_DOWN, 4)
    y_middle(3)
    z_step(ITEM_W1, 4)
    y_end(3)
    y_done(2)
    for d in (1, 2, 3):
        remote(avb.at[0], avb.at[(4 - d) % 4], av_send.at[d], av_recv.at[d], dev(z, xrel(d), y, c)).wait_recv()
    rs_far(0)
    z_step(ITEM_W2, 1, (0,))
    low_partial(2)
    z_step(ITEM_W2, 1, (1,))
    y_done(1)
    low_partial(1)
    rs_hold(0, 0)
    z_step(ITEM_W2, 2, (0,))
    rs_near(0, 0)
    y_done(3)
    low_partial(3)
    rs_hold(0, 1)
    z_step(ITEM_W2, 2, (1,))
    rs_near(0, 1)
    rs_far(1)
    low_partial(0)
    z_step(ITEM_W2, 3, (0,))
    rs_own(0)
    low_core()
    z_step(ITEM_W2, 3, (1,))
    z_start(ITEM_W3)
    rs_hold(1, 0)
    rs_near(1, 0)
    low_y()
    z_step(ITEM_W2, 4, (0,))
    rs_hold(1, 1)
    rs_near(1, 1)
    z_step(ITEM_W2, 4, (1,))
    rs_far(2)
    z_step(ITEM_W3, 1, (0,))
    low_end()
    z_step(ITEM_W3, 1, (1,))
    for d in (1, 2, 3):
        xu(d).wait_recv()
    chunk_end(0)
    z_step(ITEM_W3, 2, (0,))
    rs_own(1)
    rs_hold(2, 0)
    z_step(ITEM_W3, 2, (1,))
    rs_near(2, 0)
    rs_hold(2, 1)
    rs_near(2, 1)
    z_step(ITEM_W3, 3, (0,))
    chunk_end(1)
    z_step(ITEM_W3, 3, (1,))
    z_start(ITEM_W4)
    rs_own(2)
    z_step(ITEM_W3, 4, (0,))
    chunk_end(2)
    z_step(ITEM_W3, 4, (1,))
    rs_far(3)
    z_step(ITEM_W4, 1, (0,))
    rs_hold(3, 0)
    z_step(ITEM_W4, 1, (1,))
    rs_near(3, 0)
    rs_hold(3, 1)
    rs_near(3, 1)
    z_step(ITEM_W4, 2, (0,))
    rs_own(3)
    z_step(ITEM_W4, 2, (1,))
    z_step(ITEM_W4, 3, (0,))
    z_step(ITEM_W4, 3, (1,))
    chunk_end(3)
    z_step(ITEM_W4, 4, (0,))
    z_step(ITEM_W4, 4, (1,))
    rs_far(4)
    rs_hold(4, 0)
    rs_near(4, 0)
    rs_hold(4, 1)
    rs_near(4, 1)
    rs_own(4)
    chunk_end(4)

    for copy in sent:
        copy.wait_send()

    @pl.when(y != x)
    def _():
        remote(down.at[:, pl.ds(mo(x * 256, 256), 256)], dg.at[z, :, pl.ds(mo(y * 256, 256), 256)],
               d1_send.at[0], d1_recv.at[y], dev(z, x, x, c)).wait_send()


def shards(hidden, gain, qw, kvw, down, up_q, up_kv, lens, picks):
    half = np.arange(HEAD // 2, dtype=np.float32) * np.float32(2.0) / np.float32(HEAD)
    one = np.power(np.float32(ROPE_BASE), -half).astype(np.float32)
    freq = jnp.asarray(np.tile(np.concatenate([one, one])[None, :], (8, 1)))
    vmem, smem = pl.BlockSpec(memory_space=pltpu.VMEM), pl.BlockSpec(memory_space=pltpu.SMEM)
    dma = pltpu.SemaphoreType.DMA
    scratch = [
        pltpu.VMEM((5, 2048, 256), BF),
        pltpu.VMEM((4, T, 2048), BF),
        pltpu.VMEM((T, 1024), BF),
        pltpu.VMEM((8, 48, 1024), BF),
        pltpu.VMEM((512, 1280), BF),
        pltpu.VMEM((8, 8, T), F32),
        pltpu.VMEM((4, 8, T), F32),
        pltpu.VMEM((5, 2, 192, 256), BF),
        pltpu.VMEM((5, 2, 192, 256), BF),
        pltpu.VMEM((5, 2, T, 256), BF),
        pltpu.VMEM((5, 2, T, 256), BF),
        pltpu.VMEM((T, 256), F32),
        pltpu.VMEM((2, T, 256), F32),
        pltpu.VMEM((4, 48, T), F32),
        pltpu.VMEM((4, 48, T), F32),
        pltpu.VMEM((48, T), F32),
        pltpu.VMEM((48, T), F32),
        pltpu.VMEM((48, T), F32),
        pltpu.VMEM((4, 48, T), F32),
        pltpu.VMEM((3, T, 512), BF),
        pltpu.VMEM((T, T), F32),
        pltpu.VMEM((T, HEAD), F32),
        pltpu.VMEM((T, HEAD), F32),
        pltpu.VMEM((T, HEAD), BF),
        pltpu.VMEM((T, HEAD), BF),
        dma((112,)), dma((112,)),
        dma((20,)), dma((20,)),
        dma((4,)), dma((4,)),
        dma((4,)), dma((4,)),
        dma((4,)), dma((4,)),
        dma((8,)), dma((8,)),
        dma((4,)), dma((4,)),
        dma((20,)), dma((20,)),
        dma((8,)), dma((8,)),
        dma((1,)),
    ]
    return pl.pallas_call(
        kernel,
        out_shape=(
            jax.ShapeDtypeStruct((T, 1024), BF),
            jax.ShapeDtypeStruct((T, HEAD), BF),
            jax.ShapeDtypeStruct((T, HEAD), BF),
        ),
        in_specs=[vmem] * 8 + [smem] * 2,
        out_specs=(vmem, vmem, vmem),
        scratch_shapes=scratch,
        compiler_params=pltpu.CompilerParams(
            collective_id=0, has_side_effects=True, vmem_limit_bytes=56 * 1024 * 1024
        ),
        cost_estimate=pl.CostEstimate(flops=10_000_000_000, bytes_accessed=4_000_000, transcendentals=1_500_000),
    )(
        hidden, gain.reshape(64, 128), qw, kvw, down.reshape(48, 1024),
        up_q.reshape(16, 1024), up_kv.reshape(16, 256), freq, lens, picks,
    )


def solution(mesh):
    in_specs = (
        P("req", "blk"), P(), P("req", "blk"), P("req", "blk"), P("req", None, None, "blk"),
        P("req", None, "blk"), P("req", None, "blk"), P("req", None), P("req", None),
    )
    out_specs = (P("req", "blk"), P("req", "blk"), P("req", "blk"))
    return jax.shard_map(shards, mesh=mesh, in_specs=in_specs, out_specs=out_specs, check_vma=False)
```

```python
import functools
import math

import jax
import jax.numpy as jnp
import numpy as np
from jax import lax
from jax.experimental import pallas as pl
from jax.experimental.pallas import tpu as pltpu
from jax.sharding import PartitionSpec as P

EPSILON = 1e-05
ADAPTER_SCALE = 2.0
ROPE_BASE = 10000.0
HEAD = 128
T = 384
RANK = 16
NZ, NX, NY = 8, 4, 4
WIDTH = 8192
BF, F32 = jnp.bfloat16, jnp.float32

WIDTHS = (256, 256, 128, 128, 128, 128, 128, 128)
STARTS = tuple(sum(WIDTHS[:j]) for j in range(len(WIDTHS)))
CHUNKS = len(WIDTHS)
ITEMS = ("U", "D") + tuple(range(CHUNKS))

ORDER = (
    ("begin",), ("yb", 0), ("xs",), ("zs", 0), ("zs", 1), ("tables",), ("bias",), ("fac",), ("zw", 0, 0, 1),
    ("ym", 0, 0), ("ym", 0, 1), ("zw", 0, 1, 1), ("zs", "U"), ("ys", 0, 0), ("ys", 0, 1), ("zw", 1, 0, 1), ("yb", 2),
    ("zw", 1, 1, 1), ("sw",), ("ye", 0), ("zw", 0, 0, 2), ("yd", 0), ("yb", 1), ("zw", 0, 1, 2), ("zw", "U", 0, 1),
    ("ym", 2, 0), ("ym", 2, 1), ("zw", "U", 1, 1), ("yb", 3), ("zw", 1, 0, 2), ("ys", 2, 0), ("ys", 2, 1),
    ("zw", 1, 1, 2), ("ym", 1, 0), ("ym", 1, 1), ("zw", 0, 0, 3), ("zw", 0, 1, 3), ("zw", "U", 0, 2), ("ys", 1, 0),
    ("ys", 1, 1), ("zw", "U", 1, 2), ("zs", "D"), ("zw", 1, 0, 3), ("ye", 2), ("zw", 1, 1, 3), ("zs", 2), ("yd", 2),
    ("ym", 3, 0), ("ym", 3, 1), ("zw", 0, 0, 4), ("far", 0), ("zw", "U", 0, 3), ("own", 0), ("zw", "U", 1, 3),
    ("zs", 3), ("ys", 3, 0), ("ys", 3, 1), ("zw", "D", 0, 1), ("zw", "D", 1, 1), ("zs", 5), ("ye", 1),
    ("zw", 1, 0, 4), ("far", 1), ("own", 1), ("zw", 2, 0, 1), ("yd", 1), ("zw", 2, 1, 1), ("ye", 3), ("near", 0, 0),
    ("zw", "U", 0, 4), ("up", 1), ("up", 2), ("zw", 3, 0, 1), ("up", 3), ("yd", 3), ("zw", 3, 1, 1), ("near", 0, 1),
    ("up", 0), ("zw", "D", 0, 2), ("near", 1, 0), ("near", 1, 1), ("zw", "D", 1, 2), ("zw", 5, 0, 1), ("zw", 5, 1, 1),
    ("zw", 2, 0, 2), ("zw", 2, 1, 2), ("zw", 3, 0, 2), ("zw", 3, 1, 2), ("zw", "D", 0, 3), ("zw", "D", 1, 3),
    ("zw", 5, 0, 2), ("zw", 5, 1, 2), ("zs", 6), ("zw", 2, 0, 3), ("zw", 2, 1, 3), ("zw", 3, 0, 3), ("zw", 3, 1, 3),
    ("uw",), ("zw", "D", 0, 4), ("zs", 4), ("lp", 0), ("lp", 1), ("lp", 2), ("zw", 5, 0, 3), ("lp", 3),
    ("zw", 5, 1, 3), ("zw", 6, 0, 1), ("zw", 6, 1, 1), ("zs", 7), ("zw", 2, 0, 4), ("far", 2), ("own", 2),
    ("zw", 3, 0, 4), ("far", 3), ("own", 3), ("zw", 4, 0, 1), ("zw", 4, 1, 1), ("zw", 5, 0, 4), ("far", 5),
    ("own", 5), ("lc",), ("zw", 6, 0, 2), ("near", 2, 0), ("zw", 6, 1, 2), ("near", 2, 1), ("ly",), ("zw", 7, 0, 1),
    ("near", 3, 0), ("near", 3, 1), ("zw", 7, 1, 1), ("near", 5, 0), ("zw", 4, 0, 2), ("near", 5, 1), ("zw", 4, 1, 2),
    ("zw", 6, 0, 3), ("zw", 6, 1, 3), ("zw", 7, 0, 2), ("zw", 7, 1, 2), ("zw", 4, 0, 3), ("le",), ("zw", 4, 1, 3),
    ("end", 0, 0), ("zw", 6, 0, 4), ("far", 6), ("zw", 7, 0, 3), ("own", 6), ("end", 1, 0), ("zw", 4, 0, 4),
    ("zw", 7, 1, 3), ("far", 4), ("own", 4), ("end", 1, 1), ("zw", 7, 0, 4), ("near", 6, 0), ("near", 6, 1),
    ("far", 7), ("own", 7), ("end", 2, 0), ("near", 4, 0), ("near", 4, 1), ("end", 3, 0), ("end", 5, 0),
    ("near", 7, 0), ("near", 7, 1), ("end", 6, 0), ("end", 4, 0), ("end", 7, 0),
)


def kernel(
    hid, gain, qw, kvw, down, up_q, up_kv, freq, lens, picks,
    ctx_o, key_o, val_o,
    wg, act, raw, dg, ug, ssb, avb, gains,
    relay_s, relay_r, fin_s, fin_r, own,
    lrx_s, lrx_r, lrc_s, lrc_r, lry_s, lry_r,
    lhs, bias, cosb, sinb, keys, vals, xus, xur, usel,
    z_send, z_recv, y_send, y_recv, xa_send, xa_recv, xu_send, xu_recv,
    av_send, av_recv, ss_send, ss_recv, d1_send, d1_recv,
    rs_send, rs_recv, lr_send, lr_recv, loc_sem,
):
    b = lax.axis_index("blk")
    r = lax.axis_index("req")
    y, c = lax.div(b, 2), lax.rem(b, 2)
    z, x = lax.div(r, 4), lax.rem(r, 4)
    sgn = 1 - 2 * c

    def dev(zz, xx, yy, cc):
        return {"blk": yy * 2 + cc, "req": zz * 4 + xx}

    def zrel(d):
        return lax.rem(z + d + NZ, NZ)

    def xrel(d):
        return lax.rem(x + d + NX, NX)

    def yrel(d):
        return lax.rem(y + d + NY, NY)

    def remote(src, dst, ssem, rsem, to):
        return pltpu.make_async_remote_copy(
            src_ref=src, dst_ref=dst, send_sem=ssem, recv_sem=rsem,
            device_id=to, device_id_type=pl.DeviceIdType.MESH,
        )

    sent = []

    def go(copy):
        copy.start()
        sent.append(copy)

    def mo(v, m):
        return pl.multiple_of(v, m)

    barrier = pltpu.get_barrier_semaphore()
    peers = [dev(z, xrel(dx), yrel(dy), c) for dx in range(4) for dy in range(4) if dx or dy]
    peers += [dev(z, x, yrel(dy), 1 - c) for dy in range(4)]
    peers += [dev(zrel(1), x, y, c), dev(zrel(-1), x, y, c)]
    for peer in peers:
        pl.semaphore_signal(barrier, inc=1, device_id=peer, device_id_type=pl.DeviceIdType.MESH)

    def krow(q):
        return lax.rem(q, 2) * 4 + lax.div(q, 2)

    own_rows = pl.ds(mo(krow(z) * 256, 256), 256)
    wg[0][own_rows, :] = kvw[...]
    for j in range(1, CHUNKS):
        wg[j][own_rows, :] = qw[:, STARTS[j] - 256:STARTS[j] - 256 + WIDTHS[j]]
    up_rows = pl.ds(mo(z * 16, 16), 16)
    ug[up_rows, 0:256] = up_kv[...]
    ug[up_rows, 256:1280] = up_q[...]

    acc = None
    for i in range(8):
        v = hid[:, i * 128:(i + 1) * 128].astype(F32)
        acc = v * v if acc is None else acc + v * v
    ssb[b] = jnp.broadcast_to(jnp.sum(acc.T, axis=0, keepdims=True), (8, T))

    l0, l1, l2 = lens[0, 0], lens[0, 1], lens[0, 2]
    e0, e1, e2 = l0, l0 + l1, l0 + l1 + l2
    row_t = lax.broadcasted_iota(jnp.int32, (8, T), 1)

    def pick(t, v0, v1, v2, v3):
        return jnp.where(t < e0, v0, jnp.where(t < e1, v1, jnp.where(t < e2, v2, v3)))

    ids = pick(row_t, picks[0, 0], picks[0, 1], picks[0, 2], picks[0, 3])
    slot = row_t >> 4
    by_prompt = jnp.where(slot == 0, picks[0, 0], jnp.where(slot == 1, picks[0, 1], jnp.where(
        slot == 2, picks[0, 2], jnp.where(slot == 3, picks[0, 3], -1))))
    side_row = lax.broadcasted_iota(jnp.int32, (8, T), 0)
    avb[0, 8:16, :] = jnp.where(side_row == 0, ids, by_prompt).astype(F32)

    pl.semaphore_wait(barrier, len(peers))

    def z_slot(item, q):
        if item == "U":
            return ug.at[pl.ds(mo(q * 16, 16), 16), :]
        if item == "D":
            return dg.at[q]
        return wg[item].at[pl.ds(mo(krow(q) * 256, 256), 256), :]

    def z_copy(item, d, step):
        way = sgn if d == 0 else -sgn
        ref = z_slot(item, lax.rem(z - way * (step - 1) + NZ, NZ))
        n = (ITEMS.index(item) * 2 + d) * 4 + step - 1
        return remote(ref, ref, z_send.at[n], z_recv.at[n], dev(lax.rem(z + way + NZ, NZ), x, y, c))

    def z_start(item):
        if item == "D":
            for q in range(4):
                ref = dg.at[z, :, q * 256:(q + 1) * 256]
                remote(ref, ref, d1_send.at[0], d1_recv.at[q], dev(z, xrel(1), y, c)).wait_recv()
        for d in (0, 1):
            go(z_copy(item, d, 1))

    def z_step(item, d, step):
        way = sgn if d == 0 else -sgn
        ref = z_slot(item, lax.rem(z - way * step + NZ, NZ))
        n = (ITEMS.index(item) * 2 + d) * 4 + step - 1
        remote(ref, ref, z_send.at[n], z_recv.at[n], dev(lax.rem(z + way + NZ, NZ), x, y, c)).wait_recv()
        if step < 3 or (step == 3 and d == 0):
            go(z_copy(item, d, step + 1))

    def begin():
        for p in range(1, 8):
            dy, dc = p // 2, p % 2
            go(remote(ssb.at[b], ssb.at[b], ss_send.at[p], ss_recv.at[p],
                      dev(z, x, yrel(dy), lax.rem(c + dc, 2))))
        for d in range(4):
            def copy(d=d):
                return remote(
                    down.at[:, pl.ds(mo(xrel(d) * 256, 256), 256)],
                    dg.at[z, :, pl.ds(mo(y * 256, 256), 256)],
                    d1_send.at[d], d1_recv.at[y], dev(z, xrel(d), x, c))
            if d:
                go(copy())
            else:
                @pl.when(y == x)
                def _():
                    pltpu.make_async_copy(
                        down.at[:, pl.ds(mo(x * 256, 256), 256)],
                        dg.at[z, :, pl.ds(mo(y * 256, 256), 256)], d1_recv.at[y]).start()

                @pl.when(y != x)
                def _():
                    copy().start()

    def tables():
        col_t = lax.broadcasted_iota(jnp.int32, (T, HEAD), 0)
        position = col_t - pick(col_t, 0, e0, e1, e2)
        angles = position.astype(F32) * freq[0:1, :]
        cosb[...] = jnp.cos(angles)
        lane = lax.broadcasted_iota(jnp.int32, (T, HEAD), 1)
        sines = jnp.sin(angles)
        sinb[...] = jnp.where(lane < HEAD // 2, -sines, sines)

    def side(d):
        return remote(avb.at[0], avb.at[(4 - d) % 4], av_send.at[d], av_recv.at[d], dev(z, xrel(d), y, c))

    def factors():
        for p in range(1, 8):
            dy, dc = p // 2, p % 2
            q = yrel(-dy) * 2 + lax.rem(c + dc, 2)
            remote(ssb.at[q], ssb.at[q], ss_send.at[p], ss_recv.at[p],
                   dev(z, x, yrel(dy), lax.rem(c + dc, 2))).wait_recv()
        total = ssb[0]
        for i in range(1, 8):
            total = total + ssb[i]
        avb[0, 0:8, :] = lax.rsqrt(total / WIDTH + EPSILON)
        for d in (1, 2, 3):
            go(side(d))
        row = lax.broadcasted_iota(jnp.int32, (8, 128), 0)
        for n in range(16):
            slot, h = n // 2, n % 2
            q = (slot % 4) * 2 + slot // 4
            mine = jnp.where(row == x * 2 + h, gain[q * 8:(q + 1) * 8, :], 0.0)
            gains[0:1, n * 128:(n + 1) * 128] = jnp.sum(mine, axis=0, keepdims=True)

    def sides():
        for d in (1, 2, 3):
            side(d).wait_recv()

    def norm(k):
        if k == 0:
            own_copy.wait()
        factor = jnp.broadcast_to(avb[k, 0:1, :], (HEAD, T)).T
        for n in range(16):
            cols = slice(n * 128, (n + 1) * 128)
            act[k, :, cols] = (raw[k, :, cols].astype(F32) * factor * gains[0:1, cols]).astype(BF)

    own_cols = pl.ds(mo((c * 4 + y) * 256, 256), 256)
    quarter = pl.ds(mo(x * 256, 256), 256)

    def xa(d):
        return remote(
            hid.at[:, pl.ds(mo(xrel(d) * 256, 256), 256)], raw.at[(4 - d) % 4, :, own_cols],
            xa_send.at[d], xa_recv.at[d], dev(z, xrel(d), y, c))

    def y_cols(cc, yy):
        return pl.ds(mo((cc * 4 + yy) * 256, 256), 256)

    LOW, HIGH = slice(0, 192), slice(192, 384)

    def y_copy(k, n):
        rows = (LOW, HIGH, HIGH, LOW, LOW, HIGH, slice(0, T), slice(0, T), slice(0, T), slice(0, T))[n]
        from_y = (0, 0, 0, 0, -1, 1, 0, -1, 1, 2)[n]
        to = dev(z, x, yrel((1, 1, -1, -1, 1, -1, 0, 0, 0, 0)[n]), c if n < 6 else 1 - c)
        dst = raw.at[k, rows, y_cols(c, yrel(from_y))]
        src = hid.at[rows, quarter] if k == 0 and from_y == 0 else dst
        return remote(src, dst, y_send.at[k * 10 + n], y_recv.at[k * 10 + n], to)

    def y_wait(k, n):
        rows = (LOW, HIGH, HIGH, LOW, LOW, HIGH, slice(0, T), slice(0, T), slice(0, T), slice(0, T))[n]
        from_y = (-1, -1, 1, 1, 2, 2, 0, -1, 1, 2)[n]
        dst = raw.at[k, rows, y_cols(c if n < 6 else 1 - c, yrel(from_y))]
        remote(dst, dst, y_send.at[k * 10 + n], y_recv.at[k * 10 + n], dev(z, x, y, 1 - c)).wait_recv()

    own_copy = pltpu.make_async_copy(hid.at[:, quarter], raw.at[0, :, own_cols], loc_sem.at[0])

    def y_begin(k):
        if k:
            remote(raw.at[k, :, own_cols], raw.at[k, :, own_cols], xa_send.at[4 - k], xa_recv.at[4 - k],
                   dev(z, xrel(1), y, c)).wait_recv()
        for n in (0, 2, 1, 3, 6):
            go(y_copy(k, n))

    def y_middle(k, n):
        y_wait(k, 2 * n)
        go(y_copy(k, 4 + n))

    def y_side(k, n):
        y_wait(k, 2 * n + 1)
        go(y_copy(k, 7 + n))

    def y_end(k):
        for n in (4, 5):
            y_wait(k, n)
        go(y_copy(k, 9))

    def y_done(k):
        for n in (6, 7, 8, 9):
            y_wait(k, n)
        norm(k)

    def x_begin():
        for d in (2, 1, 3):
            go(xa(d))
        own_copy.start()

    def xu(d):
        return remote(xus.at[d], xur.at[d], xu_send.at[d], xu_recv.at[d], dev(z, xrel(d), y, c))

    def up_begin(k):
        row = lax.broadcasted_iota(jnp.int32, (128, 128), 0)
        rank = lax.broadcasted_iota(jnp.int32, (128, 128), 1) & 15
        hit = (avb[k, 9:10, 0:128] == (4 * (row >> 4) + x).astype(F32)) & ((row & 15) == rank)
        choice = jnp.where(hit, 1.0, 0.0).T[0:64].astype(BF)
        xus[k] = jnp.dot(choice, ug[...], preferred_element_type=F32).astype(BF)
        if k:
            go(xu(k))

    def up_end():
        total = xus[0].astype(F32)
        for d in (1, 2, 3):
            xu(d).wait_recv()
            total = total + xur[d].astype(F32)
        usel[...] = total.astype(BF)

    def lrx(k):
        return remote(lrx_s.at[k], lrx_r.at[k], lr_send.at[k], lr_recv.at[k], dev(z, xrel(k), y, c))

    def low_partial(k):
        part = lax.dot_general(
            dg[...].reshape(NZ * 48, 1024), act[k, :, pl.ds(mo(c * 1024, 1024), 1024)],
            (((1,), (1,)), ((), ())), preferred_element_type=F32)
        ids = avb[k, 8:9, :]
        out = None
        for q in range(NZ):
            hit = ids == (4 * q + y).astype(F32)
            term = jnp.where(hit, part[q * 48:(q + 1) * 48, :], 0.0)
            out = term if out is None else out + term
        lrx_s[k] = out
        if k:
            go(lrx(k))

    def low_core():
        total = lrx_s[0]
        for k in range(1, 4):
            lrx(k).wait_recv()
            total = total + lrx_r[k]
        lrc_s[...] = total
        go(remote(lrc_s, lrc_r, lr_send.at[4], lr_recv.at[4], dev(z, x, y, 1 - c)))

    def lry(d):
        return remote(lry_s, lry_r.at[d], lr_send.at[4 + d], lr_recv.at[4 + d], dev(z, x, yrel(d), c))

    def low_y():
        remote(lrc_s, lrc_r, lr_send.at[4], lr_recv.at[4], dev(z, x, y, 1 - c)).wait_recv()
        lry_s[...] = lrc_s[...] + lrc_r[...]
        for d in range(1, 4):
            go(lry(d))

    def low_end():
        total = lry_s[...]
        for d in range(1, 4):
            lry(d).wait_recv()
            total = total + lry_r[d]
        low = total.astype(BF)
        row = lax.broadcasted_iota(jnp.int32, (64, RANK), 0)
        rank = lax.broadcasted_iota(jnp.int32, (64, RANK), 1)
        repeat = ((row & 15) == rank).astype(BF)
        hit = (lax.broadcasted_iota(jnp.int32, (64, T), 0) >> 4) == pick(
            lax.broadcasted_iota(jnp.int32, (64, T), 1), 0, 1, 2, 3)
        for j in range(3):
            spread = jnp.dot(repeat, low[j * RANK:(j + 1) * RANK, :], preferred_element_type=F32)
            lhs[j] = jnp.where(hit, spread, 0.0).T.astype(BF)

    def make_bias():
        tc = lax.broadcasted_iota(jnp.int32, (T, T), 0)
        tr = lax.broadcasted_iota(jnp.int32, (T, T), 1)
        allowed = (pick(tc, 0, 1, 2, 3) == pick(tr, 0, 1, 2, 3)) & (tr <= tc)
        bias[...] = jnp.where(allowed, 0.0, -1e30)

    def part(k, j):
        return jnp.dot(act[k], wg[j][...], preferred_element_type=F32)

    def relay(j, d):
        return remote(relay_s[j].at[d], relay_r[j].at[d], rs_send.at[j * 4 + d], rs_recv.at[j * 4 + d],
                      dev(z, xrel(1 - 2 * d), y, c))

    def final(j, d):
        return remote(fin_s[j].at[d], fin_r[j].at[d], rs_send.at[j * 4 + 2 + d], rs_recv.at[j * 4 + 2 + d],
                      dev(z, xrel(1 - 2 * d), y, c))

    def rs_far(j):
        p = part(2, j).astype(BF)
        for d in (0, 1):
            relay_s[j][d] = p[d * 192:(d + 1) * 192]
            go(relay(j, d))

    def rs_near(j, d):
        p = part(1 if d == 0 else 3, j)
        relay(j, d).wait_recv()
        lo = d * 192
        fin_s[j][d, lo:lo + 192] = (p[lo:lo + 192] + relay_r[j][d].astype(F32)).astype(BF)
        fin_s[j][d, 192 - lo:384 - lo] = p[192 - lo:384 - lo].astype(BF)
        go(final(j, d))

    def rs_own(j):
        own[j][...] = part(0, j)

    def rotate(v):
        return v * cosb[...] + pltpu.roll(v, HEAD // 2, axis=1) * sinb[...]

    def chunk_end(j, i):
        if i == 0:
            for d in (0, 1):
                final(j, d).wait_recv()
        cols = slice(i * 128, (i + 1) * 128) if j else slice(0, 256)
        base = own[j][:, cols]
        for d in (0, 1):
            base = base + fin_r[j][d, :, cols].astype(F32)
        if j == 0:
            k = base[:, 0:128] + ADAPTER_SCALE * jnp.dot(lhs[1], usel[:, 0:128], preferred_element_type=F32)
            v = base[:, 128:256] + ADAPTER_SCALE * jnp.dot(lhs[2], usel[:, 128:256], preferred_element_type=F32)
            k, v = rotate(k).astype(BF), v.astype(BF)
            keys[...] = k
            vals[...] = v
            key_o[...] = k
            val_o[...] = v
            return
        lo = STARTS[j] + i * 128
        base = base + ADAPTER_SCALE * jnp.dot(lhs[0], usel[:, lo:lo + 128], preferred_element_type=F32)
        q = rotate(base).astype(BF)
        for n in range(3):
            rows, wide = slice(n * 128, (n + 1) * 128), (n + 1) * 128
            s = lax.dot_general(q[rows], keys[0:wide, :], (((1,), (1,)), ((), ())), preferred_element_type=F32)
            s = s * (1.0 / math.sqrt(HEAD)) + bias[rows, 0:wide]
            e = jnp.exp(s - jnp.max(s, axis=1, keepdims=True))
            a = (e / jnp.sum(e, axis=1, keepdims=True)).astype(BF)
            o = jnp.dot(a, vals[0:wide, :], preferred_element_type=F32)
            ctx_o[rows, lo - 256:lo - 128] = o.astype(BF)

    steps = {
        "begin": begin, "tables": tables, "fac": factors, "sw": sides, "uw": up_end, "bias": make_bias,
        "zs": z_start, "zw": z_step, "xs": x_begin, "yb": y_begin, "ym": y_middle, "ys": y_side, "ye": y_end, "yd": y_done,
        "up": up_begin, "lp": low_partial, "lc": low_core, "ly": low_y, "le": low_end,
        "far": rs_far, "near": rs_near, "own": rs_own, "end": chunk_end,
    }
    for name, *arguments in ORDER:
        steps[name](*arguments)

    for copy in sent:
        copy.wait_send()

    @pl.when(y != x)
    def _():
        remote(down.at[:, pl.ds(mo(x * 256, 256), 256)], dg.at[z, :, pl.ds(mo(y * 256, 256), 256)],
               d1_send.at[0], d1_recv.at[y], dev(z, x, x, c)).wait_send()


def hand_over(ctx, key, val, ctx_o, key_o, val_o):
    ctx_o[...] = ctx[...]
    key_o[...] = key[...]
    val_o[...] = val[...]


def shards(hidden, gain, qw, kvw, down, up_q, up_kv, lens, picks):
    half = np.arange(HEAD // 2, dtype=np.float32) * np.float32(2.0) / np.float32(HEAD)
    one = np.power(np.float32(ROPE_BASE), -half).astype(np.float32)
    freq = jnp.asarray(np.tile(np.concatenate([one, one])[None, :], (8, 1)))
    vmem, smem = pl.BlockSpec(memory_space=pltpu.VMEM), pl.BlockSpec(memory_space=pltpu.SMEM)
    dma = pltpu.SemaphoreType.DMA
    scratch = [
        [pltpu.VMEM((2048, w), BF) for w in WIDTHS],
        pltpu.VMEM((4, T, 2048), BF),
        pltpu.VMEM((4, T, 2048), BF),
        pltpu.VMEM((8, 48, 1024), BF),
        pltpu.VMEM((128, 1280), BF),
        pltpu.VMEM((8, 8, T), F32),
        pltpu.VMEM((4, 16, T), F32),
        pltpu.VMEM((8, 2048), F32),
        [pltpu.VMEM((2, 192, w), BF) for w in WIDTHS],
        [pltpu.VMEM((2, 192, w), BF) for w in WIDTHS],
        [pltpu.VMEM((2, T, w), BF) for w in WIDTHS],
        [pltpu.VMEM((2, T, w), BF) for w in WIDTHS],
        [pltpu.VMEM((T, w), F32) for w in WIDTHS],
        pltpu.VMEM((4, 48, T), F32),
        pltpu.VMEM((4, 48, T), F32),
        pltpu.VMEM((48, T), F32),
        pltpu.VMEM((48, T), F32),
        pltpu.VMEM((48, T), F32),
        pltpu.VMEM((4, 48, T), F32),
        pltpu.VMEM((3, T, 64), BF),
        pltpu.VMEM((T, T), F32),
        pltpu.VMEM((T, HEAD), F32),
        pltpu.VMEM((T, HEAD), F32),
        pltpu.VMEM((T, HEAD), BF),
        pltpu.VMEM((T, HEAD), BF),
        pltpu.VMEM((4, 64, 1280), BF),
        pltpu.VMEM((4, 64, 1280), BF),
        pltpu.VMEM((64, 1280), BF),
        dma((8 * len(ITEMS),)), dma((8 * len(ITEMS),)),
        dma((40,)), dma((40,)),
        dma((4,)), dma((4,)),
        dma((4,)), dma((4,)),
        dma((4,)), dma((4,)),
        dma((8,)), dma((8,)),
        dma((4,)), dma((4,)),
        dma((4 * CHUNKS,)), dma((4 * CHUNKS,)),
        dma((8,)), dma((8,)),
        dma((1,)),
    ]
    context, keys, values = pl.pallas_call(
        kernel,
        out_shape=(
            jax.ShapeDtypeStruct((T, 1024), BF),
            jax.ShapeDtypeStruct((T, HEAD), BF),
            jax.ShapeDtypeStruct((T, HEAD), BF),
        ),
        in_specs=[vmem] * 8 + [smem] * 2,
        out_specs=(vmem, vmem, vmem),
        scratch_shapes=scratch,
        compiler_params=pltpu.CompilerParams(
            collective_id=0, has_side_effects=True, vmem_limit_bytes=56 * 1024 * 1024
        ),
        cost_estimate=pl.CostEstimate(flops=10_000_000_000, bytes_accessed=4_000_000, transcendentals=1_500_000),
    )(
        hidden, gain.reshape(64, 128), qw, kvw, down.reshape(48, 1024),
        up_q.reshape(16, 1024), up_kv.reshape(16, 256), freq, lens, picks,
    )
    shapes = tuple(jax.ShapeDtypeStruct(a.shape, a.dtype) for a in (context, keys, values))
    return pl.pallas_call(
        hand_over, out_shape=shapes, in_specs=[vmem] * 3, out_specs=(vmem,) * 3,
    )(context, keys, values)


def solution(mesh):
    in_specs = (
        P("req", "blk"), P(), P("req", "blk"), P("req", "blk"), P("req", None, None, "blk"),
        P("req", None, "blk"), P("req", None, "blk"), P("req", None), P("req", None),
    )
    out_specs = (P("req", "blk"), P("req", "blk"), P("req", "blk"))
    return jax.shard_map(shards, mesh=mesh, in_specs=in_specs, out_specs=out_specs, check_vma=False)
```

```python
import functools
import math

import jax
import jax.numpy as jnp
import numpy as np
from jax import lax
from jax.experimental import pallas as pl
from jax.experimental.pallas import tpu as pltpu
from jax.sharding import PartitionSpec as P

EPSILON = 1e-05
ADAPTER_SCALE = 2.0
ROPE_BASE = 10000.0
HEAD = 128
T = 384
RANK = 16
NZ, NX, NY = 8, 4, 4
WIDTH = 8192
BF, F32 = jnp.bfloat16, jnp.float32

WIDTHS = (256, 256, 128, 128, 128, 128, 128, 128)
STARTS = tuple(sum(WIDTHS[:j]) for j in range(len(WIDTHS)))
CHUNKS = len(WIDTHS)
ITEMS = ("U", "D") + tuple(range(CHUNKS))

ORDER = (
    ("begin",), ("yb", 0), ("xs",), ("zs", "U"), ("zs", 0), ("tables",), ("bias",), ("zw", "U", 0, 1),
    ("zw", "U", 1, 1), ("fac",), ("zs", 1), ("ym", 0, 0), ("ym", 0, 1), ("zw", 0, 0, 1), ("zw", 0, 1, 1), ("zs", 2),
    ("ys", 0, 0), ("ys", 0, 1), ("zw", "U", 0, 2), ("zw", "U", 1, 2), ("yb", 2), ("sw",), ("zw", 1, 0, 1), ("ye", 0),
    ("zw", 1, 1, 1), ("yd", 0), ("zw", 0, 0, 2), ("ym", 2, 0), ("ym", 2, 1), ("yb", 1), ("zw", 0, 1, 2),
    ("zw", 2, 0, 1), ("ys", 2, 0), ("ys", 2, 1), ("zw", 2, 1, 1), ("zw", "U", 0, 3), ("zw", "U", 1, 3), ("ye", 2),
    ("zw", 1, 0, 2), ("yd", 2), ("zw", 1, 1, 2), ("zs", 3), ("ym", 1, 0), ("ym", 1, 1), ("yb", 3), ("zw", 0, 0, 3),
    ("ys", 1, 0), ("ys", 1, 1), ("zw", 0, 1, 3), ("zw", 2, 0, 2), ("zw", 2, 1, 2), ("zs", "D"), ("zw", "U", 0, 4),
    ("up", 1), ("up", 2), ("ye", 1), ("up", 3), ("up", 0), ("zw", 1, 0, 3), ("yd", 1), ("ym", 3, 0), ("ym", 3, 1),
    ("zw", 1, 1, 3), ("zw", 3, 0, 1), ("zw", 3, 1, 1), ("ys", 3, 0), ("ys", 3, 1), ("zw", 0, 0, 4), ("far", 0),
    ("own", 0), ("zw", 2, 0, 3), ("ye", 3), ("zw", 2, 1, 3), ("zw", "D", 0, 1), ("yd", 3), ("zw", "D", 1, 1), ("uw",),
    ("zw", 1, 0, 4), ("zs", 4), ("far", 1), ("zw", 3, 0, 2), ("own", 1), ("near", 0, 0), ("zw", 3, 1, 2),
    ("near", 0, 1), ("zw", 2, 0, 4), ("far", 2), ("own", 2), ("zw", "D", 0, 2), ("zw", "D", 1, 2), ("zs", 6),
    ("zw", 4, 0, 1), ("near", 1, 0), ("zw", 4, 1, 1), ("near", 1, 1), ("zw", 3, 0, 3), ("zw", 3, 1, 3),
    ("zw", "D", 0, 3), ("zw", "D", 1, 3), ("zw", 6, 0, 1), ("near", 2, 0), ("zw", 6, 1, 1), ("near", 2, 1),
    ("zw", 4, 0, 2), ("zw", 4, 1, 2), ("zw", 3, 0, 4), ("far", 3), ("own", 3), ("zw", "D", 0, 4), ("zs", 7),
    ("lp", 0), ("lp", 1), ("zw", 6, 0, 2), ("lp", 2), ("lp", 3), ("zw", 6, 1, 2), ("zw", 4, 0, 3), ("zw", 4, 1, 3),
    ("zs", 5), ("zw", 7, 0, 1), ("near", 3, 0), ("zw", 7, 1, 1), ("near", 3, 1), ("zw", 6, 0, 3), ("zw", 6, 1, 3),
    ("zw", 4, 0, 4), ("far", 4), ("own", 4), ("zw", 5, 0, 1), ("lc",), ("zw", 5, 1, 1), ("zw", 7, 0, 2), ("ly",),
    ("zw", 7, 1, 2), ("zw", 6, 0, 4), ("far", 6), ("near", 4, 0), ("zw", 5, 0, 2), ("near", 4, 1), ("zw", 5, 1, 2),
    ("own", 6), ("zw", 7, 0, 3), ("zw", 7, 1, 3), ("near", 6, 0), ("zw", 5, 0, 3), ("near", 6, 1), ("zw", 5, 1, 3),
    ("le",), ("zw", 7, 0, 4), ("far", 7), ("end", 0, 0), ("own", 7), ("zw", 5, 0, 4), ("far", 5), ("own", 5),
    ("end", 1, 0), ("end", 1, 1), ("near", 7, 0), ("near", 7, 1), ("near", 5, 0), ("near", 5, 1), ("end", 2, 0),
    ("end", 3, 0), ("end", 4, 0), ("end", 6, 0), ("end", 7, 0), ("end", 5, 0),
)


def kernel(
    hid, gain, qw, kvw, down, up_q, up_kv, freq, lens, picks,
    ctx_o, key_o, val_o,
    wg, act, raw, dg, ug, ssb, avb, gains,
    relay_s, relay_r, fin_s, fin_r, own,
    lrx_s, lrx_r, lrc_s, lrc_r, lry_s, lry_r,
    lhs, bias, cosb, sinb, keys, vals, xus, xur, usel,
    z_send, z_recv, y_send, y_recv, xa_send, xa_recv, xu_send, xu_recv,
    av_send, av_recv, ss_send, ss_recv, d1_send, d1_recv,
    rs_send, rs_recv, lr_send, lr_recv, loc_sem,
):
    b = lax.axis_index("blk")
    r = lax.axis_index("req")
    y, c = lax.div(b, 2), lax.rem(b, 2)
    z, x = lax.div(r, 4), lax.rem(r, 4)
    sgn = 1 - 2 * c

    def dev(zz, xx, yy, cc):
        return {"blk": yy * 2 + cc, "req": zz * 4 + xx}

    def zrel(d):
        return lax.rem(z + d + NZ, NZ)

    def xrel(d):
        return lax.rem(x + d + NX, NX)

    def yrel(d):
        return lax.rem(y + d + NY, NY)

    def remote(src, dst, ssem, rsem, to):
        return pltpu.make_async_remote_copy(
            src_ref=src, dst_ref=dst, send_sem=ssem, recv_sem=rsem,
            device_id=to, device_id_type=pl.DeviceIdType.MESH,
        )

    sent = []

    def go(copy):
        copy.start()
        sent.append(copy)

    def mo(v, m):
        return pl.multiple_of(v, m)

    barrier = pltpu.get_barrier_semaphore()
    peers = [dev(z, xrel(dx), yrel(dy), c) for dx in range(4) for dy in range(4) if dx or dy]
    peers += [dev(z, x, yrel(dy), 1 - c) for dy in range(4)]
    peers += [dev(zrel(1), x, y, c), dev(zrel(-1), x, y, c)]
    for peer in peers:
        pl.semaphore_signal(barrier, inc=1, device_id=peer, device_id_type=pl.DeviceIdType.MESH)

    def krow(q):
        return lax.rem(q, 2) * 4 + lax.div(q, 2)

    own_rows = pl.ds(mo(krow(z) * 256, 256), 256)
    wg[0][own_rows, :] = kvw[...]
    for j in range(1, CHUNKS):
        wg[j][own_rows, :] = qw[:, STARTS[j] - 256:STARTS[j] - 256 + WIDTHS[j]]
    up_rows = pl.ds(mo(z * 16, 16), 16)
    ug[up_rows, 0:256] = up_kv[...]
    ug[up_rows, 256:1280] = up_q[...]

    acc = None
    for i in range(8):
        v = hid[:, i * 128:(i + 1) * 128].astype(F32)
        acc = v * v if acc is None else acc + v * v
    ssb[b] = jnp.broadcast_to(jnp.sum(acc.T, axis=0, keepdims=True), (8, T))

    l0, l1, l2 = lens[0, 0], lens[0, 1], lens[0, 2]
    e0, e1, e2 = l0, l0 + l1, l0 + l1 + l2
    row_t = lax.broadcasted_iota(jnp.int32, (8, T), 1)

    def pick(t, v0, v1, v2, v3):
        return jnp.where(t < e0, v0, jnp.where(t < e1, v1, jnp.where(t < e2, v2, v3)))

    ids = pick(row_t, picks[0, 0], picks[0, 1], picks[0, 2], picks[0, 3])
    slot = row_t >> 4
    by_prompt = jnp.where(slot == 0, picks[0, 0], jnp.where(slot == 1, picks[0, 1], jnp.where(
        slot == 2, picks[0, 2], jnp.where(slot == 3, picks[0, 3], -1))))
    side_row = lax.broadcasted_iota(jnp.int32, (8, T), 0)
    avb[0, 8:16, :] = jnp.where(side_row == 0, ids, by_prompt).astype(F32)

    pl.semaphore_wait(barrier, len(peers))

    def z_slot(item, q):
        if item == "U":
            return ug.at[pl.ds(mo(q * 16, 16), 16), :]
        if item == "D":
            return dg.at[q]
        return wg[item].at[pl.ds(mo(krow(q) * 256, 256), 256), :]

    def z_copy(item, d, step):
        way = sgn if d == 0 else -sgn
        ref = z_slot(item, lax.rem(z - way * (step - 1) + NZ, NZ))
        n = (ITEMS.index(item) * 2 + d) * 4 + step - 1
        return remote(ref, ref, z_send.at[n], z_recv.at[n], dev(lax.rem(z + way + NZ, NZ), x, y, c))

    def z_start(item):
        if item == "D":
            for q in range(4):
                ref = dg.at[z, :, q * 256:(q + 1) * 256]
                remote(ref, ref, d1_send.at[0], d1_recv.at[q], dev(z, xrel(1), y, c)).wait_recv()
        for d in (0, 1):
            go(z_copy(item, d, 1))

    def z_step(item, d, step):
        way = sgn if d == 0 else -sgn
        ref = z_slot(item, lax.rem(z - way * step + NZ, NZ))
        n = (ITEMS.index(item) * 2 + d) * 4 + step - 1
        remote(ref, ref, z_send.at[n], z_recv.at[n], dev(lax.rem(z + way + NZ, NZ), x, y, c)).wait_recv()
        if step < 3 or (step == 3 and d == 0):
            go(z_copy(item, d, step + 1))

    def begin():
        for p in range(1, 8):
            dy, dc = p // 2, p % 2
            go(remote(ssb.at[b], ssb.at[b], ss_send.at[p], ss_recv.at[p],
                      dev(z, x, yrel(dy), lax.rem(c + dc, 2))))
        for d in range(4):
            def copy(d=d):
                return remote(
                    down.at[:, pl.ds(mo(xrel(d) * 256, 256), 256)],
                    dg.at[z, :, pl.ds(mo(y * 256, 256), 256)],
                    d1_send.at[d], d1_recv.at[y], dev(z, xrel(d), x, c))
            if d:
                go(copy())
            else:
                @pl.when(y == x)
                def _():
                    pltpu.make_async_copy(
                        down.at[:, pl.ds(mo(x * 256, 256), 256)],
                        dg.at[z, :, pl.ds(mo(y * 256, 256), 256)], d1_recv.at[y]).start()

                @pl.when(y != x)
                def _():
                    copy().start()

    def tables():
        col_t = lax.broadcasted_iota(jnp.int32, (T, HEAD), 0)
        position = col_t - pick(col_t, 0, e0, e1, e2)
        angles = position.astype(F32) * freq[0:1, :]
        cosb[...] = jnp.cos(angles)
        lane = lax.broadcasted_iota(jnp.int32, (T, HEAD), 1)
        sines = jnp.sin(angles)
        sinb[...] = jnp.where(lane < HEAD // 2, -sines, sines)

    def side(d):
        return remote(avb.at[0], avb.at[(4 - d) % 4], av_send.at[d], av_recv.at[d], dev(z, xrel(d), y, c))

    def factors():
        for p in range(1, 8):
            dy, dc = p // 2, p % 2
            q = yrel(-dy) * 2 + lax.rem(c + dc, 2)
            remote(ssb.at[q], ssb.at[q], ss_send.at[p], ss_recv.at[p],
                   dev(z, x, yrel(dy), lax.rem(c + dc, 2))).wait_recv()
        total = ssb[0]
        for i in range(1, 8):
            total = total + ssb[i]
        avb[0, 0:8, :] = lax.rsqrt(total / WIDTH + EPSILON)
        for d in (1, 2, 3):
            go(side(d))
        row = lax.broadcasted_iota(jnp.int32, (8, 128), 0)
        for n in range(16):
            slot, h = n // 2, n % 2
            q = (slot % 4) * 2 + slot // 4
            mine = jnp.where(row == x * 2 + h, gain[q * 8:(q + 1) * 8, :], 0.0)
            gains[0:1, n * 128:(n + 1) * 128] = jnp.sum(mine, axis=0, keepdims=True)

    def sides():
        for d in (1, 2, 3):
            side(d).wait_recv()

    def norm(k):
        if k == 0:
            own_copy.wait()
        factor = jnp.broadcast_to(avb[k, 0:1, :], (HEAD, T)).T
        for n in range(16):
            cols = slice(n * 128, (n + 1) * 128)
            act[k, :, cols] = (raw[k, :, cols].astype(F32) * factor * gains[0:1, cols]).astype(BF)

    own_cols = pl.ds(mo((c * 4 + y) * 256, 256), 256)
    quarter = pl.ds(mo(x * 256, 256), 256)

    def xa(d):
        return remote(
            hid.at[:, pl.ds(mo(xrel(d) * 256, 256), 256)], raw.at[(4 - d) % 4, :, own_cols],
            xa_send.at[d], xa_recv.at[d], dev(z, xrel(d), y, c))

    def y_cols(cc, yy):
        return pl.ds(mo((cc * 4 + yy) * 256, 256), 256)

    LOW, HIGH = slice(0, 192), slice(192, 384)

    def y_copy(k, n):
        rows = (LOW, HIGH, HIGH, LOW, LOW, HIGH, slice(0, T), slice(0, T), slice(0, T), slice(0, T))[n]
        from_y = (0, 0, 0, 0, -1, 1, 0, -1, 1, 2)[n]
        to = dev(z, x, yrel((1, 1, -1, -1, 1, -1, 0, 0, 0, 0)[n]), c if n < 6 else 1 - c)
        dst = raw.at[k, rows, y_cols(c, yrel(from_y))]
        src = hid.at[rows, quarter] if k == 0 and from_y == 0 else dst
        return remote(src, dst, y_send.at[k * 10 + n], y_recv.at[k * 10 + n], to)

    def y_wait(k, n):
        rows = (LOW, HIGH, HIGH, LOW, LOW, HIGH, slice(0, T), slice(0, T), slice(0, T), slice(0, T))[n]
        from_y = (-1, -1, 1, 1, 2, 2, 0, -1, 1, 2)[n]
        dst = raw.at[k, rows, y_cols(c if n < 6 else 1 - c, yrel(from_y))]
        remote(dst, dst, y_send.at[k * 10 + n], y_recv.at[k * 10 + n], dev(z, x, y, 1 - c)).wait_recv()

    own_copy = pltpu.make_async_copy(hid.at[:, quarter], raw.at[0, :, own_cols], loc_sem.at[0])

    def y_begin(k):
        if k:
            remote(raw.at[k, :, own_cols], raw.at[k, :, own_cols], xa_send.at[4 - k], xa_recv.at[4 - k],
                   dev(z, xrel(1), y, c)).wait_recv()
        for n in (0, 2, 1, 3, 6):
            go(y_copy(k, n))

    def y_middle(k, n):
        y_wait(k, 2 * n)
        go(y_copy(k, 4 + n))

    def y_side(k, n):
        y_wait(k, 2 * n + 1)
        go(y_copy(k, 7 + n))

    def y_end(k):
        for n in (4, 5):
            y_wait(k, n)
        go(y_copy(k, 9))

    def y_done(k):
        for n in (6, 7, 8, 9):
            y_wait(k, n)
        norm(k)

    def x_begin():
        for d in (2, 1, 3):
            go(xa(d))
        own_copy.start()

    def xu(d):
        return remote(xus.at[d], xur.at[d], xu_send.at[d], xu_recv.at[d], dev(z, xrel(d), y, c))

    def up_begin(k):
        row = lax.broadcasted_iota(jnp.int32, (128, 128), 0)
        rank = lax.broadcasted_iota(jnp.int32, (128, 128), 1) & 15
        hit = (avb[k, 9:10, 0:128] == (4 * (row >> 4) + x).astype(F32)) & ((row & 15) == rank)
        choice = jnp.where(hit, 1.0, 0.0).T[0:64].astype(BF)
        xus[k] = jnp.dot(choice, ug[...], preferred_element_type=F32).astype(BF)
        if k:
            go(xu(k))

    def up_end():
        total = xus[0].astype(F32)
        for d in (1, 2, 3):
            xu(d).wait_recv()
            total = total + xur[d].astype(F32)
        usel[...] = total.astype(BF)

    def lrx(k):
        return remote(lrx_s.at[k], lrx_r.at[k], lr_send.at[k], lr_recv.at[k], dev(z, xrel(k), y, c))

    def low_partial(k):
        part = lax.dot_general(
            dg[...].reshape(NZ * 48, 1024), act[k, :, pl.ds(mo(c * 1024, 1024), 1024)],
            (((1,), (1,)), ((), ())), preferred_element_type=F32)
        ids = avb[k, 8:9, :]
        out = None
        for q in range(NZ):
            hit = ids == (4 * q + y).astype(F32)
            term = jnp.where(hit, part[q * 48:(q + 1) * 48, :], 0.0)
            out = term if out is None else out + term
        lrx_s[k] = out
        if k:
            go(lrx(k))

    def low_core():
        total = lrx_s[0]
        for k in range(1, 4):
            lrx(k).wait_recv()
            total = total + lrx_r[k]
        lrc_s[...] = total
        go(remote(lrc_s, lrc_r, lr_send.at[4], lr_recv.at[4], dev(z, x, y, 1 - c)))

    def lry(d):
        return remote(lry_s, lry_r.at[d], lr_send.at[4 + d], lr_recv.at[4 + d], dev(z, x, yrel(d), c))

    def low_y():
        remote(lrc_s, lrc_r, lr_send.at[4], lr_recv.at[4], dev(z, x, y, 1 - c)).wait_recv()
        lry_s[...] = lrc_s[...] + lrc_r[...]
        for d in range(1, 4):
            go(lry(d))

    def low_end():
        total = lry_s[...]
        for d in range(1, 4):
            lry(d).wait_recv()
            total = total + lry_r[d]
        low = total.astype(BF)
        row = lax.broadcasted_iota(jnp.int32, (64, RANK), 0)
        rank = lax.broadcasted_iota(jnp.int32, (64, RANK), 1)
        repeat = ((row & 15) == rank).astype(BF)
        hit = (lax.broadcasted_iota(jnp.int32, (64, T), 0) >> 4) == pick(
            lax.broadcasted_iota(jnp.int32, (64, T), 1), 0, 1, 2, 3)
        for j in range(3):
            spread = jnp.dot(repeat, low[j * RANK:(j + 1) * RANK, :], preferred_element_type=F32)
            lhs[j] = jnp.where(hit, spread, 0.0).T.astype(BF)

    def make_bias():
        tc = lax.broadcasted_iota(jnp.int32, (T, T), 0)
        tr = lax.broadcasted_iota(jnp.int32, (T, T), 1)
        allowed = (pick(tc, 0, 1, 2, 3) == pick(tr, 0, 1, 2, 3)) & (tr <= tc)
        bias[...] = jnp.where(allowed, 0.0, -1e30)

    def part(k, j):
        return jnp.dot(act[k], wg[j][...], preferred_element_type=F32)

    def relay(j, d):
        return remote(relay_s[j].at[d], relay_r[j].at[d], rs_send.at[j * 4 + d], rs_recv.at[j * 4 + d],
                      dev(z, xrel(1 - 2 * d), y, c))

    def final(j, d):
        return remote(fin_s[j].at[d], fin_r[j].at[d], rs_send.at[j * 4 + 2 + d], rs_recv.at[j * 4 + 2 + d],
                      dev(z, xrel(1 - 2 * d), y, c))

    def rs_far(j):
        p = part(2, j).astype(BF)
        for d in (0, 1):
            relay_s[j][d] = p[d * 192:(d + 1) * 192]
            go(relay(j, d))

    def rs_near(j, d):
        p = part(1 if d == 0 else 3, j)
        relay(j, d).wait_recv()
        lo = d * 192
        fin_s[j][d, lo:lo + 192] = (p[lo:lo + 192] + relay_r[j][d].astype(F32)).astype(BF)
        fin_s[j][d, 192 - lo:384 - lo] = p[192 - lo:384 - lo].astype(BF)
        go(final(j, d))

    def rs_own(j):
        own[j][...] = part(0, j)

    def rotate(v):
        return v * cosb[...] + pltpu.roll(v, HEAD // 2, axis=1) * sinb[...]

    def chunk_end(j, i):
        if i == 0:
            for d in (0, 1):
                final(j, d).wait_recv()
        cols = slice(i * 128, (i + 1) * 128) if j else slice(0, 256)
        base = own[j][:, cols]
        for d in (0, 1):
            base = base + fin_r[j][d, :, cols].astype(F32)
        if j == 0:
            k = base[:, 0:128] + ADAPTER_SCALE * jnp.dot(lhs[1], usel[:, 0:128], preferred_element_type=F32)
            v = base[:, 128:256] + ADAPTER_SCALE * jnp.dot(lhs[2], usel[:, 128:256], preferred_element_type=F32)
            k, v = rotate(k).astype(BF), v.astype(BF)
            keys[...] = k
            vals[...] = v
            key_o[...] = k
            val_o[...] = v
            return
        lo = STARTS[j] + i * 128
        base = base + ADAPTER_SCALE * jnp.dot(lhs[0], usel[:, lo:lo + 128], preferred_element_type=F32)
        q = rotate(base).astype(BF)
        for n in range(3):
            rows, wide = slice(n * 128, (n + 1) * 128), (n + 1) * 128
            s = lax.dot_general(q[rows], keys[0:wide, :], (((1,), (1,)), ((), ())), preferred_element_type=F32)
            s = s * (1.0 / math.sqrt(HEAD)) + bias[rows, 0:wide]
            e = jnp.exp(s - jnp.max(s, axis=1, keepdims=True))
            a = (e * (1.0 / jnp.sum(e, axis=1, keepdims=True))).astype(BF)
            o = jnp.dot(a, vals[0:wide, :], preferred_element_type=F32)
            ctx_o[rows, lo - 256:lo - 128] = o.astype(BF)

    steps = {
        "begin": begin, "tables": tables, "fac": factors, "sw": sides, "uw": up_end, "bias": make_bias,
        "zs": z_start, "zw": z_step, "xs": x_begin, "yb": y_begin, "ym": y_middle, "ys": y_side, "ye": y_end, "yd": y_done,
        "up": up_begin, "lp": low_partial, "lc": low_core, "ly": low_y, "le": low_end,
        "far": rs_far, "near": rs_near, "own": rs_own, "end": chunk_end,
    }
    for name, *arguments in ORDER:
        steps[name](*arguments)

    for copy in sent:
        copy.wait_send()

    @pl.when(y != x)
    def _():
        remote(down.at[:, pl.ds(mo(x * 256, 256), 256)], dg.at[z, :, pl.ds(mo(y * 256, 256), 256)],
               d1_send.at[0], d1_recv.at[y], dev(z, x, x, c)).wait_send()


def hand_over(ctx, key, val, ctx_o, key_o, val_o):
    ctx_o[...] = ctx[...]
    key_o[...] = key[...]
    val_o[...] = val[...]


def shards(hidden, gain, qw, kvw, down, up_q, up_kv, lens, picks):
    half = np.arange(HEAD // 2, dtype=np.float32) * np.float32(2.0) / np.float32(HEAD)
    one = np.power(np.float32(ROPE_BASE), -half).astype(np.float32)
    freq = jnp.asarray(np.tile(np.concatenate([one, one])[None, :], (8, 1)))
    vmem, smem = pl.BlockSpec(memory_space=pltpu.VMEM), pl.BlockSpec(memory_space=pltpu.SMEM)
    dma = pltpu.SemaphoreType.DMA
    scratch = [
        [pltpu.VMEM((2048, w), BF) for w in WIDTHS],
        pltpu.VMEM((4, T, 2048), BF),
        pltpu.VMEM((4, T, 2048), BF),
        pltpu.VMEM((8, 48, 1024), BF),
        pltpu.VMEM((128, 1280), BF),
        pltpu.VMEM((8, 8, T), F32),
        pltpu.VMEM((4, 16, T), F32),
        pltpu.VMEM((8, 2048), F32),
        [pltpu.VMEM((2, 192, w), BF) for w in WIDTHS],
        [pltpu.VMEM((2, 192, w), BF) for w in WIDTHS],
        [pltpu.VMEM((2, T, w), BF) for w in WIDTHS],
        [pltpu.VMEM((2, T, w), BF) for w in WIDTHS],
        [pltpu.VMEM((T, w), F32) for w in WIDTHS],
        pltpu.VMEM((4, 48, T), F32),
        pltpu.VMEM((4, 48, T), F32),
        pltpu.VMEM((48, T), F32),
        pltpu.VMEM((48, T), F32),
        pltpu.VMEM((48, T), F32),
        pltpu.VMEM((4, 48, T), F32),
        pltpu.VMEM((3, T, 64), BF),
        pltpu.VMEM((T, T), F32),
        pltpu.VMEM((T, HEAD), F32),
        pltpu.VMEM((T, HEAD), F32),
        pltpu.VMEM((T, HEAD), BF),
        pltpu.VMEM((T, HEAD), BF),
        pltpu.VMEM((4, 64, 1280), BF),
        pltpu.VMEM((4, 64, 1280), BF),
        pltpu.VMEM((64, 1280), BF),
        dma((8 * len(ITEMS),)), dma((8 * len(ITEMS),)),
        dma((40,)), dma((40,)),
        dma((4,)), dma((4,)),
        dma((4,)), dma((4,)),
        dma((4,)), dma((4,)),
        dma((8,)), dma((8,)),
        dma((4,)), dma((4,)),
        dma((4 * CHUNKS,)), dma((4 * CHUNKS,)),
        dma((8,)), dma((8,)),
        dma((1,)),
    ]
    context, keys, values = pl.pallas_call(
        kernel,
        out_shape=(
            jax.ShapeDtypeStruct((T, 1024), BF),
            jax.ShapeDtypeStruct((T, HEAD), BF),
            jax.ShapeDtypeStruct((T, HEAD), BF),
        ),
        in_specs=[vmem] * 8 + [smem] * 2,
        out_specs=(vmem, vmem, vmem),
        scratch_shapes=scratch,
        compiler_params=pltpu.CompilerParams(
            collective_id=0, has_side_effects=True, vmem_limit_bytes=56 * 1024 * 1024
        ),
        cost_estimate=pl.CostEstimate(flops=10_000_000_000, bytes_accessed=4_000_000, transcendentals=1_500_000),
    )(
        hidden, gain.reshape(64, 128), qw, kvw, down.reshape(48, 1024),
        up_q.reshape(16, 1024), up_kv.reshape(16, 256), freq, lens, picks,
    )
    shapes = tuple(jax.ShapeDtypeStruct(a.shape, a.dtype) for a in (context, keys, values))
    return pl.pallas_call(
        hand_over, out_shape=shapes, in_specs=[vmem] * 3, out_specs=(vmem,) * 3,
    )(context, keys, values)


def solution(mesh):
    in_specs = (
        P("req", "blk"), P(), P("req", "blk"), P("req", "blk"), P("req", None, None, "blk"),
        P("req", None, "blk"), P("req", None, "blk"), P("req", None), P("req", None),
    )
    out_specs = (P("req", "blk"), P("req", "blk"), P("req", "blk"))
    return jax.shard_map(shards, mesh=mesh, in_specs=in_specs, out_specs=out_specs, check_vma=False)
```
